32 devices in a mesh: groups: 2 (over x), wide: 16 (over z, y, core).
Axes of the slice: x: 2, y: 2, z: 4, core: 2. Of those that a mesh axis runs over, the one named last changes fastest.
Arguments:
- embeds: bfloat16 [32768, 768], P(('groups', 'wide')), parts along dimension 0
- labels: int32 [32768], P(('groups', 'wide')), parts along dimension 0, may hold values from 0 to 63, as said below
Outputs:
- average: bfloat16 [32768, 768], P(('groups', 'wide')), parts along dimension 0
- density: bfloat16 [32768], P(('groups', 'wide')), parts along dimension 0
The draws below stay inside these ranges and needn't reach their ends.
There are 2 independent parts, one for each index of `groups`. The reference program is written for one: setup_inputs(seed, part) draws one part's arguments, and reference() takes and returns one part's arrays. A program takes and returns all parts, laid end to end along the dimension named above; each array names one. Nothing has to cross between parts.
Inputs may be any that keep to these rules, and one draw needn't show every extreme that they name: `labels`: cluster c is local cluster c % 4 of owner c // 4. Of the rows of one device, at most 128 have clusters of one owner, and on every device some owner gets exactly 128.
All inputs are finite; a program needn't handle non-finite values.
Results may differ from the reference program's by a relative error of at most 0.0034.
Values may be sent and summed in bfloat16 or wider, within the bound.
A program may use at most 64 MiB of HBM per device.

```python
import jax
import jax.numpy as jnp
from jax import lax

D = 768
ROWS_DEV = 1024
CL_DEV = 4
CAP = 128
ROWS = 16384
CLUSTERS = 64
N_WIDE = 16


def routing(key):
    total = N_WIDE * CAP

    def device_rows(sub):
        first, second, third = jax.random.split(sub, 3)
        chosen_owner = jax.random.randint(first, (), 0, N_WIDE)
        places = jnp.arange(total, dtype=jnp.int32)
        ranks = jax.random.permutation(second, total).astype(jnp.int32)
        score = jnp.where(places // CAP == chosen_owner, ranks - total, ranks)
        order = jnp.argsort(score)[:ROWS_DEV].astype(jnp.int32)
        dest = order // CAP
        local = jax.random.randint(third, (ROWS_DEV,), 0, CL_DEV)
        return (dest * CL_DEV + local).astype(jnp.int32)
    keys = jax.random.split(jax.random.fold_in(key, 102), N_WIDE)
    return jax.vmap(device_rows)(keys).reshape(ROWS).astype(jnp.int32)


def draw_labels(key, part):
    return routing(key)


def build_rows(key, labels, src_lo, src_hi, eps_lo, eps_hi):
    sources_per = max(2, ROWS_DEV // (CL_DEV * 8))
    total_src = CLUSTERS * sources_per
    keys = jax.random.split(key, 6)
    centers = jax.random.normal(keys[0], (CLUSTERS, D), jnp.float32)
    src_spread = jnp.exp(jax.random.uniform(keys[1], (total_src, 1), jnp.float32, jnp.log(src_lo), jnp.log(src_hi)))
    src_noise = jax.random.normal(keys[2], (total_src, D), jnp.float32)
    owner_center = jnp.arange(total_src, dtype=jnp.int32) // sources_per
    sources = centers[owner_center] + src_spread * src_noise
    pick = jax.random.randint(keys[3], (ROWS,), 0, sources_per).astype(jnp.int32)
    base = sources[labels * sources_per + pick]
    row_eps = jnp.exp(jax.random.uniform(keys[4], (ROWS, 1), jnp.float32, jnp.log(eps_lo), jnp.log(eps_hi)))
    row_noise = jax.random.normal(keys[5], (ROWS, D), jnp.float32)
    return base + row_eps * row_noise


def draw_embeds(key, part):
    labels = routing(key)
    key = jax.random.fold_in(key, 7)
    values = build_rows(key, labels, 0.6, 1.3, 0.12, 0.6)
    return values.astype(jnp.bfloat16)


def setup_inputs(seed: int = 0, part: int = 0) -> dict:
    streams_of = jax.random.split(jax.random.key(seed), 3)
    part_keys = jax.random.split(jax.random.fold_in(streams_of[2], part), 3)
    embeds = draw_embeds(jax.random.fold_in(jax.random.fold_in(streams_of[2], part), 71), part)
    labels = draw_labels(jax.random.fold_in(jax.random.fold_in(streams_of[2], part), 71), part)
    return {"embeds": embeds, "labels": labels}


TAU = 0.2

def cluster_block(rows, tag):
    count = rows.shape[0]
    blk = min(512, count)
    qrows = rows.reshape(count // blk, blk, rows.shape[1])
    qtag = tag.reshape(count // blk, blk)

    def one(item):
        query, qt = item
        sim = jnp.dot(query, rows.T, preferred_element_type=jnp.float32)
        same = (qt[:, None] == tag[None, :]) & (tag[None, :] > 0)
        weight = jnp.where(same, jnp.exp((sim - 1.0) / TAU), 0.0)
        dens = lax.optimization_barrier(jnp.sum(weight, axis=1))
        dens = jnp.where(qt > 0, dens, 1.0)
        numer = jnp.dot(weight.astype(jnp.bfloat16), rows, preferred_element_type=jnp.float32)
        return ((numer / dens[:, None]).astype(jnp.bfloat16), dens.astype(jnp.bfloat16))
    avg, dens = lax.map(one, (qrows, qtag))
    return (avg.reshape(count, rows.shape[1]), dens.reshape(count))

def reference(embeds, labels):
    x = embeds.astype(jnp.float32)
    squared = lax.optimization_barrier(jnp.sum(x * x, axis=1, keepdims=True))
    inside = squared + 1e-06
    unit = (x * lax.rsqrt(inside)).astype(jnp.bfloat16)
    owner = labels // CL_DEV
    local = labels % CL_DEV
    slots_all = N_WIDE * CAP

    def one(owner_id, carry):
        avg_all, dens_all = carry
        mask = owner == owner_id
        count = jnp.sum(mask.astype(jnp.int32))
        index = jnp.nonzero(mask, size=slots_all, fill_value=0)[0].astype(jnp.int32)
        live = jnp.arange(slots_all, dtype=jnp.int32) < count
        rows = unit[index]
        tag = jnp.where(live, local[index] + 1, 0).astype(jnp.int32)
        avg, dens = cluster_block(rows, tag)
        target = jnp.where(live, index, ROWS).astype(jnp.int32)
        avg_all = avg_all.at[target].set(avg, mode='drop')
        dens_all = dens_all.at[target].set(dens, mode='drop')
        return (avg_all, dens_all)
    init = (jnp.zeros((ROWS, D), jnp.bfloat16), jnp.zeros((ROWS,), jnp.bfloat16))
    average, density = lax.fori_loop(0, N_WIDE, one, init)
    return (average, density)
```

```python
import functools
import math

import jax
import jax.numpy as jnp
from jax import lax
from jax.experimental import pallas as pl
from jax.experimental.pallas import tpu as pltpu
from jax.sharding import PartitionSpec as P

CL_DEV = 4
TAU = 0.2
SCALE = math.log2(math.e) / TAU
TILE = 256
F32 = jnp.float32
BF16 = jnp.bfloat16


def kernel(n, embeds, labels, out, out_dens,
           unit, send, recv, back, home, numer, total,
           stag, rtag, bden, hden, ktag, qtag, dacc, pos, pos_t,
           s_rows, r_rows, s_tags, r_tags, s_back, r_back, s_den, r_den):
    rows, width = embeds.shape
    cap = 2 * rows // n
    slots = n * cap
    tiles = slots // TILE
    per_tile = TILE // cap
    per_lane = 128 // cap
    me = lax.axis_index("wide")

    barrier = pltpu.get_barrier_semaphore()

    @pl.loop(1, n)
    def _(k):
        pl.semaphore_signal(barrier, inc=1, device_id={"wide": lax.rem(me + k, n)},
                            device_id_type=pl.DeviceIdType.MESH)

    def to_dest(k):
        return {"wide": lax.rem(me + k, n)}

    def to_source(k):
        return {"wide": lax.rem(me - k + n, n)}

    def slot_rows(k):
        return pl.ds(pl.multiple_of(k * cap, cap), cap)

    def slot_tags(k):
        return pl.ds(pl.multiple_of(k * 8, 8), 8)

    def remote(src, dst, ssem, rsem, where):
        return pltpu.make_async_remote_copy(
            src_ref=src, dst_ref=dst, send_sem=ssem, recv_sem=rsem,
            device_id=where, device_id_type=pl.DeviceIdType.MESH)

    def go_rows(k):
        return remote(send.at[slot_rows(k)], recv.at[slot_rows(k)], s_rows.at[k], r_rows.at[k], to_dest(k))

    def go_tags(k):
        return remote(stag.at[slot_tags(k)], rtag.at[slot_tags(k)], s_tags.at[k], r_tags.at[k], to_dest(k))

    def back_rows(k):
        return remote(back.at[slot_rows(k)], home.at[slot_rows(k)], s_back.at[k], r_back.at[k], to_source(k))

    def back_dens(k):
        return remote(bden.at[slot_tags(k)], hden.at[slot_tags(k)], s_den.at[k], r_den.at[k], to_source(k))

    def tile_of(t):
        return pl.ds(pl.multiple_of(t * TILE, TILE), TILE)

    @pl.loop(0, rows // 128)
    def _(b):
        at = pl.ds(pl.multiple_of(b * 128, 128), 128)
        x = embeds[at, :].astype(F32)
        inside = jnp.sum(x * x, axis=1, keepdims=True) + 1e-06
        unit[at, :] = (x * lax.rsqrt(inside)).astype(BF16)

    lab = labels[...]
    ahead = (lab >> 2) - me
    ahead = jnp.where(ahead < 0, ahead + n, ahead)
    tag = ((lab & 3) + 1).astype(F32)
    which = lax.broadcasted_iota(jnp.int32, (n, TILE), 0)
    before = (lax.broadcasted_iota(jnp.int32, (TILE, TILE), 0)
              < lax.broadcasted_iota(jnp.int32, (TILE, TILE), 1)).astype(F32).astype(BF16)
    running = jnp.zeros((n, 1), F32)
    for b in range(rows // TILE):
        piece = ahead[:, b * TILE:(b + 1) * TILE]
        hot = (jnp.broadcast_to(piece, (n, TILE)) == which).astype(F32)
        rank = jnp.dot(hot.astype(BF16), before, preferred_element_type=F32) + running
        running = running + jnp.sum(hot, axis=1, keepdims=True)
        rank = jnp.sum(hot * rank, axis=0, keepdims=True)
        pos[:, b * TILE:(b + 1) * TILE] = jnp.broadcast_to(
            rank + (piece * cap).astype(F32), (8, TILE))

    tag8 = jnp.broadcast_to(tag, (8, rows)).astype(BF16)
    lane = lax.broadcasted_iota(jnp.int32, (8, 128), 1)

    def picks(t):
        ids = (lax.broadcasted_iota(jnp.int32, (TILE, rows), 0) + t * TILE).astype(F32)
        return jnp.where(ids == pos[0:1, :], 1.0, 0.0).astype(BF16)

    def own_lanes(piece, j):
        if per_lane == 1:
            return piece
        low = (j % per_lane) * cap
        return jnp.where((lane >= low) & (lane < low + cap), piece, 0.0)

    def pack(t):
        sel = picks(t)
        send[tile_of(t), :] = jnp.dot(sel, unit[...], preferred_element_type=F32).astype(BF16)
        tags = lax.dot_general(tag8, sel, (((1,), (1,)), ((), ())), preferred_element_type=F32)
        for j in range(per_tile):
            at = j // per_lane * 128
            stag[slot_tags(t * per_tile + j), :] = own_lanes(tags[:, at:at + 128], j)

    def launch(t, first):
        for j in range(first, per_tile):
            go_rows(t * per_tile + j).start()
            go_tags(t * per_tile + j).start()

    pack(0)
    pl.semaphore_wait(barrier, n - 1)
    launch(0, 1)
    recv[0:cap, :] = send[0:cap, :]
    rtag[0:8, :] = stag[0:8, :]

    @pl.loop(1, tiles)
    def _(t):
        pack(t)
        launch(t, 0)

    pos_t[...] = jnp.broadcast_to(pos[0:1, :], (128, rows)).T

    def arrive(t, first):
        for j in range(first, per_tile):
            go_rows(t * per_tile + j).wait_recv()
            go_tags(t * per_tile + j).wait_recv()
        halves = []
        for h in range(TILE // 128):
            tags = rtag[slot_tags(t * per_tile + h * per_lane), :]
            for j in range(1, per_lane):
                tags = tags + rtag[slot_tags(t * per_tile + h * per_lane + j), :]
            halves.append(tags)
        both = jnp.concatenate(halves, axis=1)
        ktag[pl.ds(pl.multiple_of(t * 8, 8), 8), :] = jnp.where(both > 0.0, both, -1.0)
        qtag[tile_of(t), :] = jnp.broadcast_to(both[0:1, :], (128, TILE)).T

    def pair(i, j, fresh=False):
        query, keys = recv[tile_of(i), :], recv[tile_of(j), :]
        sim = lax.dot_general(query, keys, (((1,), (1,)), ((), ())), preferred_element_type=F32)
        left = qtag[tile_of(i), :]
        right = ktag[pl.ds(pl.multiple_of(j * 8, 8), 8), :][0:1, :]
        same = jnp.concatenate([left, left], axis=1) == right
        weight = jnp.where(same, jnp.exp2((sim - 1.0) * SCALE), 0.0)
        dens = weight[:, :128] + weight[:, 128:]
        num = jnp.dot(weight.astype(BF16), keys, preferred_element_type=F32)
        if fresh:
            dacc[tile_of(i), :] = dens
            numer[tile_of(i), :] = num
        else:
            dacc[tile_of(i), :] += dens
            numer[tile_of(i), :] += num

    arrive(0, 1)
    pair(0, 0, True)

    @pl.loop(1, tiles - 1)
    def _(t):
        arrive(t, 0)
        pair(t, t, True)

        @pl.loop(0, t)
        def _(i):
            pair(i, t)
            pair(t, i)

    def finish(t):
        dens = jnp.sum(dacc[tile_of(t), :], axis=1, keepdims=True)
        dens = jnp.where(qtag[tile_of(t), :] > 0.0, dens, 1.0)
        inv = 1.0 / dens
        back[tile_of(t), :] = (
            numer[tile_of(t), :] * jnp.concatenate([inv] * (width // 128), axis=1)).astype(BF16)
        turned = dens.T[0:8, :]
        for j in range(per_tile):
            at = j // per_lane * 128
            bden[slot_tags(t * per_tile + j), :] = own_lanes(turned[:, at:at + 128], j)

    def give(t, first):
        for j in range(first, per_tile):
            back_rows(t * per_tile + j).start()
            back_dens(t * per_tile + j).start()

    last = tiles - 1
    arrive(last, 0)
    pair(last, last, True)
    pair(0, last)
    finish(0)
    give(0, 1)
    home[0:cap, :] = back[0:cap, :]
    hden[0:8, :] = bden[0:8, :]

    @pl.loop(1, last)
    def _(i):
        pair(i, last)
        finish(i)
        give(i, 0)

    @pl.loop(0, last)
    def _(i):
        pair(last, i)

    finish(last)
    give(last, 0)

    def collect(t, first):
        for j in range(first, per_tile):
            back_rows(t * per_tile + j).wait_recv()
            back_dens(t * per_tile + j).wait_recv()
        halves = []
        for h in range(TILE // 128):
            den = hden[slot_tags(t * per_tile + h * per_lane), :]
            for j in range(1, per_lane):
                den = den + hden[slot_tags(t * per_tile + h * per_lane + j), :]
            halves.append(den)
        den = jnp.concatenate(halves, axis=1).astype(BF16)
        den = jnp.dot(den, picks(t), preferred_element_type=F32)
        came = home[tile_of(t), :]
        ids = (lax.broadcasted_iota(jnp.int32, (TILE, TILE), 1) + t * TILE).astype(F32)
        return came, ids, den

    def place(b, came, ids):
        here = pos_t[tile_of(b), :]
        sel = jnp.where(ids == jnp.concatenate([here, here], axis=1), 1.0, 0.0).astype(BF16)
        return jnp.dot(sel, came, preferred_element_type=F32)

    came, ids, den = collect(0, 1)
    out_dens[...] = den
    for b in range(rows // TILE):
        total[tile_of(b), :] = place(b, came, ids)

    @pl.loop(1, last)
    def _(t):
        came, ids, den = collect(t, 0)
        out_dens[...] += den
        for b in range(rows // TILE):
            total[tile_of(b), :] += place(b, came, ids)

    came, ids, den = collect(last, 0)
    out_dens[...] += den
    for b in range(rows // TILE):
        out[tile_of(b), :] = (total[tile_of(b), :] + place(b, came, ids)).astype(BF16)

    @pl.loop(1, n)
    def _(k):
        go_rows(k).wait_send()
        go_tags(k).wait_send()
        back_rows(k).wait_send()
        back_dens(k).wait_send()


def per_device(embeds, labels):
    rows, width = embeds.shape
    n = lax.axis_size("wide")
    slots = 2 * rows
    vmem = pl.BlockSpec(memory_space=pltpu.VMEM)
    average, dens = pl.pallas_call(
        functools.partial(kernel, n),
        out_shape=(jax.ShapeDtypeStruct((rows, width), BF16),
                   jax.ShapeDtypeStruct((8, rows), F32)),
        in_specs=[vmem, vmem],
        out_specs=(vmem, vmem),
        scratch_shapes=[
            pltpu.VMEM((rows, width), BF16),
            pltpu.VMEM((slots, width), BF16),
            pltpu.VMEM((slots, width), BF16),
            pltpu.VMEM((slots, width), BF16),
            pltpu.VMEM((slots, width), BF16),
            pltpu.VMEM((slots, width), F32),
            pltpu.VMEM((rows, width), F32),
            pltpu.VMEM((n * 8, 128), F32),
            pltpu.VMEM((n * 8, 128), F32),
            pltpu.VMEM((n * 8, 128), F32),
            pltpu.VMEM((n * 8, 128), F32),
            pltpu.VMEM((slots // TILE * 8, TILE), F32),
            pltpu.VMEM((slots, 128), F32),
            pltpu.VMEM((slots, 128), F32),
            pltpu.VMEM((8, rows), F32),
            pltpu.VMEM((rows, 128), F32),
        ] + [pltpu.SemaphoreType.DMA((n,))] * 8,
        compiler_params=pltpu.CompilerParams(
            collective_id=0, has_side_effects=True, vmem_limit_bytes=52 * 1024 * 1024),
        cost_estimate=pl.CostEstimate(
            flops=4 * slots * slots * width + 8 * rows * slots * width,
            bytes_accessed=4 * rows * width, transcendentals=slots * slots),
    )(embeds, labels.reshape(1, rows))
    return average, dens[0].astype(BF16)


def solution(mesh):
    placed = (P(("groups", "wide"), None), P(("groups", "wide")))
    return jax.shard_map(
        per_device,
        mesh=mesh,
        in_specs=placed,
        out_specs=(P(("groups", "wide"), None), P(("groups", "wide"))),
        check_vma=False,
    )
```

```python
import functools
import math

import jax
import jax.numpy as jnp
from jax import lax
from jax.experimental import pallas as pl
from jax.experimental.pallas import tpu as pltpu
from jax.sharding import PartitionSpec as P

CL_DEV = 4
TAU = 0.2
SCALE = math.log2(math.e) / TAU
TILE = 256
F32 = jnp.float32
BF16 = jnp.bfloat16


def kernel(n, embeds, labels, out, out_dens,
           unit, send, recv, back, home, numer, total,
           stag, rtag, bden, hden, ktag, qtag, dacc, pos, pos_t,
           s_rows, r_rows, s_tags, r_tags, s_back, r_back, s_den, r_den):
    rows, width = embeds.shape
    cap = 2 * rows // n
    slots = n * cap
    tiles = slots // TILE
    per_tile = TILE // cap
    per_lane = 128 // cap
    me = lax.axis_index("wide")

    barrier = pltpu.get_barrier_semaphore()

    @pl.loop(1, n)
    def _(k):
        pl.semaphore_signal(barrier, inc=1, device_id={"wide": lax.rem(me + k, n)},
                            device_id_type=pl.DeviceIdType.MESH)

    def to_dest(k):
        return {"wide": lax.rem(me + k, n)}

    def to_source(k):
        return {"wide": lax.rem(me - k + n, n)}

    def slot_rows(k):
        return pl.ds(pl.multiple_of(k * cap, cap), cap)

    def slot_tags(k):
        return pl.ds(pl.multiple_of(k * 8, 8), 8)

    def remote(src, dst, ssem, rsem, where):
        return pltpu.make_async_remote_copy(
            src_ref=src, dst_ref=dst, send_sem=ssem, recv_sem=rsem,
            device_id=where, device_id_type=pl.DeviceIdType.MESH)

    def go_rows(k):
        return remote(send.at[slot_rows(k)], recv.at[slot_rows(k)], s_rows.at[k], r_rows.at[k], to_dest(k))

    def go_tags(k):
        return remote(stag.at[slot_tags(k)], rtag.at[slot_tags(k)], s_tags.at[k], r_tags.at[k], to_dest(k))

    def back_rows(k):
        return remote(back.at[slot_rows(k)], home.at[slot_rows(k)], s_back.at[k], r_back.at[k], to_source(k))

    def back_dens(k):
        return remote(bden.at[slot_tags(k)], hden.at[slot_tags(k)], s_den.at[k], r_den.at[k], to_source(k))

    def tile_of(t):
        return pl.ds(pl.multiple_of(t * TILE, TILE), TILE)

    @pl.loop(0, rows // 128)
    def _(b):
        at = pl.ds(pl.multiple_of(b * 128, 128), 128)
        x = embeds[at, :].astype(F32)
        inside = jnp.sum(x * x, axis=1, keepdims=True) + 1e-06
        unit[at, :] = (x * lax.rsqrt(inside)).astype(BF16)

    lab = labels[...]
    ahead = (lab >> 2) - me
    ahead = jnp.where(ahead < 0, ahead + n, ahead)
    tag = ((lab & 3) + 1).astype(F32)
    which = lax.broadcasted_iota(jnp.int32, (n, TILE), 0)
    before = (lax.broadcasted_iota(jnp.int32, (TILE, TILE), 0)
              < lax.broadcasted_iota(jnp.int32, (TILE, TILE), 1)).astype(F32).astype(BF16)
    running = jnp.zeros((n, 1), F32)
    for b in range(rows // TILE):
        piece = ahead[:, b * TILE:(b + 1) * TILE]
        hot = (jnp.broadcast_to(piece, (n, TILE)) == which).astype(F32)
        rank = jnp.dot(hot.astype(BF16), before, preferred_element_type=F32) + running
        running = running + jnp.sum(hot, axis=1, keepdims=True)
        rank = jnp.sum(hot * rank, axis=0, keepdims=True)
        pos[:, b * TILE:(b + 1) * TILE] = jnp.broadcast_to(
            rank + (piece * cap).astype(F32), (8, TILE))

    tag8 = jnp.broadcast_to(tag, (8, rows)).astype(BF16)
    lane = lax.broadcasted_iota(jnp.int32, (8, 128), 1)

    def picks(t):
        ids = (lax.broadcasted_iota(jnp.int32, (TILE, rows), 0) + t * TILE).astype(F32)
        return jnp.where(ids == pos[0:1, :], 1.0, 0.0).astype(BF16)

    def own_lanes(piece, j):
        if per_lane == 1:
            return piece
        low = (j % per_lane) * cap
        return jnp.where((lane >= low) & (lane < low + cap), piece, 0.0)

    def pack(t):
        sel = picks(t)
        send[tile_of(t), :] = jnp.dot(sel, unit[...], preferred_element_type=F32).astype(BF16)
        tags = lax.dot_general(tag8, sel, (((1,), (1,)), ((), ())), preferred_element_type=F32)
        for j in range(per_tile):
            at = j // per_lane * 128
            stag[slot_tags(t * per_tile + j), :] = own_lanes(tags[:, at:at + 128], j)

    def launch(t, first):
        for j in range(first, per_tile):
            go_rows(t * per_tile + j).start()
            go_tags(t * per_tile + j).start()

    pack(0)
    pl.semaphore_wait(barrier, n - 1)
    launch(0, 1)
    recv[0:cap, :] = send[0:cap, :]
    rtag[0:8, :] = stag[0:8, :]

    @pl.loop(1, tiles)
    def _(t):
        pack(t)
        launch(t, 0)

    pos_t[...] = jnp.broadcast_to(pos[0:1, :], (128, rows)).T

    def arrive(t, first):
        for j in range(first, per_tile):
            go_rows(t * per_tile + j).wait_recv()
            go_tags(t * per_tile + j).wait_recv()
        halves = []
        for h in range(TILE // 128):
            tags = rtag[slot_tags(t * per_tile + h * per_lane), :]
            for j in range(1, per_lane):
                tags = tags + rtag[slot_tags(t * per_tile + h * per_lane + j), :]
            halves.append(tags)
        both = jnp.concatenate(halves, axis=1)
        ktag[pl.ds(pl.multiple_of(t * 8, 8), 8), :] = jnp.where(both > 0.0, both, -1.0)
        qtag[tile_of(t), :] = jnp.broadcast_to(both[0:1, :], (128, TILE)).T

    def pair(i, j, fresh=False):
        query, keys = recv[tile_of(i), :], recv[tile_of(j), :]
        sim = lax.dot_general(query, keys, (((1,), (1,)), ((), ())), preferred_element_type=F32)
        left = qtag[tile_of(i), :]
        right = ktag[pl.ds(pl.multiple_of(j * 8, 8), 8), :][0:1, :]
        same = jnp.concatenate([left, left], axis=1) == right
        weight = jnp.where(same, jnp.exp2((sim - 1.0) * SCALE), 0.0)
        dens = weight[:, :128] + weight[:, 128:]
        num = jnp.dot(weight.astype(BF16), keys, preferred_element_type=F32)
        if fresh:
            dacc[tile_of(i), :] = dens
            numer[tile_of(i), :] = num
        else:
            dacc[tile_of(i), :] += dens
            numer[tile_of(i), :] += num

    arrive(0, 1)
    pair(0, 0, True)

    @pl.loop(1, tiles - 1)
    def _(t):
        arrive(t, 0)
        pair(t, t, True)

        @pl.loop(0, t)
        def _(i):
            pair(i, t)
            pair(t, i)

    def finish(t):
        dens = jnp.sum(dacc[tile_of(t), :], axis=1, keepdims=True)
        dens = jnp.where(qtag[tile_of(t), :] > 0.0, dens, 1.0)
        inv = 1.0 / dens
        back[tile_of(t), :] = (
            numer[tile_of(t), :] * jnp.concatenate([inv] * (width // 128), axis=1)).astype(BF16)
        turned = dens.T[0:8, :]
        for j in range(per_tile):
            at = j // per_lane * 128
            bden[slot_tags(t * per_tile + j), :] = own_lanes(turned[:, at:at + 128], j)

    def give(t, first):
        for j in range(first, per_tile):
            back_rows(t * per_tile + j).start()
            back_dens(t * per_tile + j).start()

    last = tiles - 1
    arrive(last, 0)
    pair(last, last, True)
    pair(0, last)
    finish(0)
    give(0, 1)
    home[0:cap, :] = back[0:cap, :]
    hden[0:8, :] = bden[0:8, :]

    @pl.loop(1, last)
    def _(i):
        pair(i, last)
        finish(i)
        give(i, 0)

    @pl.loop(0, last)
    def _(i):
        pair(last, i)

    finish(last)
    give(last, 0)

    def collect(t, first):
        for j in range(first, per_tile):
            back_rows(t * per_tile + j).wait_recv()
            back_dens(t * per_tile + j).wait_recv()
        halves = []
        for h in range(TILE // 128):
            den = hden[slot_tags(t * per_tile + h * per_lane), :]
            for j in range(1, per_lane):
                den = den + hden[slot_tags(t * per_tile + h * per_lane + j), :]
            halves.append(den)
        den = jnp.concatenate(halves, axis=1).astype(BF16)
        den = jnp.dot(den, picks(t), preferred_element_type=F32)
        came = home[tile_of(t), :]
        ids = (lax.broadcasted_iota(jnp.int32, (TILE, TILE), 1) + t * TILE).astype(F32)
        return came, ids, den

    def place(b, came, ids):
        here = pos_t[tile_of(b), :]
        sel = jnp.where(ids == jnp.concatenate([here, here], axis=1), 1.0, 0.0).astype(BF16)
        return jnp.dot(sel, came, preferred_element_type=F32)

    came, ids, den = collect(0, 1)
    out_dens[...] = den
    for b in range(rows // TILE):
        total[tile_of(b), :] = place(b, came, ids)

    @pl.loop(1, last)
    def _(t):
        came, ids, den = collect(t, 0)
        out_dens[...] += den
        for b in range(rows // TILE):
            total[tile_of(b), :] += place(b, came, ids)

    came, ids, den = collect(last, 0)
    out_dens[...] += den
    for b in range(rows // TILE):
        out[tile_of(b), :] = (total[tile_of(b), :] + place(b, came, ids)).astype(BF16)

    @pl.loop(1, n)
    def _(k):
        go_rows(k).wait_send()
        go_tags(k).wait_send()
        back_rows(k).wait_send()
        back_dens(k).wait_send()


def fast_kernel(n, groups, embeds, labels, out, out_dens, out_flag,
                unit, send, recv, back, home, numer, total,
                stag, rtag, bden, hden, ktag, qtag, dacc, pos, pos_t,
                mtag, tsum, dmat, hsum, otag1, otag2, oden2, oden1, obuf, osum, fin, ssend1, ssend2, flags,
                s_rows, r_rows, s_tags, r_tags, s_back, r_back, s_den, r_den,
                s_o1, r_o1, s_o1t, r_o1t, s_o2, r_o2, s_o2t, r_o2t,
                s_b2, r_b2, s_b2d, r_b2d, s_b1, r_b1, s_b1d, r_b1d, s_f, r_f):
    rows, width = embeds.shape
    cap = 2 * rows // n
    direct = 3 * cap // 4
    extra = cap // 4
    layer = 4
    half = n // 2 * direct
    gap = n * extra
    slots = 2 * rows
    tiles = slots // TILE
    spare = gap // layer
    chunks = slots // 128
    me = lax.axis_index("wide")
    mine = lax.axis_index("groups") * n + me
    everyone = groups * n
    floor, spot = me // layer, lax.rem(me, layer)

    barrier = pltpu.get_barrier_semaphore()

    def nth(q):
        who = lax.rem(q + everyone, everyone)
        return {"groups": who // n, "wide": lax.rem(who, n)}

    @pl.loop(1, everyone)
    def _(q):
        pl.semaphore_signal(barrier, inc=1, device_id=nth(mine + q), device_id_type=pl.DeviceIdType.MESH)

    def to_dest(k):
        return {"wide": lax.rem(me + k, n)}

    def to_source(k):
        return {"wide": lax.rem(me - k + n, n)}

    def across(i):
        return {"wide": floor * layer + lax.rem(spot + i + layer, layer)}

    def slot_rows(k):
        return pl.ds(pl.multiple_of(k * direct + k // (n // 2) * gap, 32), direct)

    def eights(k):
        return pl.ds(pl.multiple_of(k * 8, 8), 8)

    def marks(k):
        return pl.ds(pl.multiple_of(k * chunks, 8), chunks)

    def tile_of(t):
        return pl.ds(pl.multiple_of(t * TILE, TILE), TILE)

    def over(i):
        return pl.ds(half + i * spare, spare)

    def part(j):
        return pl.ds(half + j * extra, extra)

    def remote(src, dst, ssem, rsem, where):
        return pltpu.make_async_remote_copy(
            src_ref=src, dst_ref=dst, send_sem=ssem, recv_sem=rsem,
            device_id=where, device_id_type=pl.DeviceIdType.MESH)

    def go_rows(k):
        return remote(send.at[slot_rows(k)], recv.at[slot_rows(k)], s_rows.at[k], r_rows.at[k], to_dest(k))

    def go_tags(k):
        return remote(stag.at[marks(k)], rtag.at[marks(k)], s_tags.at[k], r_tags.at[k], to_dest(k))

    def back_rows(k):
        return remote(back.at[slot_rows(k)], home.at[slot_rows(k)], s_back.at[k], r_back.at[k], to_source(k))

    def back_dens(k):
        return remote(bden.at[marks(k)], hden.at[marks(k)], s_den.at[k], r_den.at[k], to_source(k))

    def one_rows(j):
        return remote(send.at[part(0)], recv.at[part(j)], s_o1.at[j], r_o1.at[j], to_dest(layer * j))

    def one_tags(j):
        return remote(ssend1.at[eights(j)], otag1.at[eights(j)], s_o1t.at[j], r_o1t.at[j], to_dest(layer * j))

    def two_rows(i):
        return remote(recv.at[over(0)], recv.at[over(i)], s_o2.at[i], r_o2.at[i], across(i))

    def two_tags(i):
        return remote(otag2.at[eights(0)], otag2.at[eights(i)], s_o2t.at[i], r_o2t.at[i], across(i))

    def three_rows(i):
        return remote(back.at[over(i)], obuf.at[pl.ds(i * spare, spare)], s_b2.at[i], r_b2.at[i], across(-i))

    def three_dens(i):
        return remote(ssend2.at[eights(i)], oden2.at[eights(i)], s_b2d.at[i], r_b2d.at[i], across(-i))

    def four_rows(j):
        return remote(osum.at[pl.ds(j * extra, extra)], fin.at[pl.ds(j * extra, extra)],
                      s_b1.at[j], r_b1.at[j], to_source(layer * j))

    def four_dens(j):
        return remote(ssend1.at[eights(layer + j)], oden1.at[eights(j)], s_b1d.at[j], r_b1d.at[j],
                      to_source(layer * j))

    def tell(q):
        return remote(flags.at[eights(0)], flags.at[eights(q)], s_f.at[q], r_f.at[q], nth(mine + q))

    @pl.loop(0, rows // 128)
    def _(b):
        at = pl.ds(pl.multiple_of(b * 128, 128), 128)
        x = embeds[at, :].astype(F32)
        inside = jnp.sum(x * x, axis=1, keepdims=True) + 1e-06
        unit[at, :] = (x * lax.rsqrt(inside)).astype(BF16)

    lab = labels[...]
    ahead = (lab >> 2) - me
    ahead = jnp.where(ahead < 0, ahead + n, ahead)
    which = lax.broadcasted_iota(jnp.int32, (n, TILE), 0)
    before = (lax.broadcasted_iota(jnp.int32, (TILE, TILE), 0)
              < lax.broadcasted_iota(jnp.int32, (TILE, TILE), 1)).astype(F32).astype(BF16)
    running = jnp.zeros((n, 1), F32)
    beyond = jnp.zeros((8, 1), F32)
    for b in range(rows // TILE):
        piece = ahead[:, b * TILE:(b + 1) * TILE]
        hot = (jnp.broadcast_to(piece, (n, TILE)) == which).astype(F32)
        rank = jnp.dot(hot.astype(BF16), before, preferred_element_type=F32) + running
        running = running + jnp.sum(hot, axis=1, keepdims=True)
        rank = jnp.broadcast_to(jnp.sum(hot * rank, axis=0, keepdims=True), (8, TILE))
        base = jnp.broadcast_to(
            (piece * direct + jnp.where(piece >= n // 2, gap, 0)).astype(F32), (8, TILE))
        past = jnp.where(rank >= direct, 1.0, 0.0)
        late = jnp.dot(past.astype(BF16), before, preferred_element_type=F32) + beyond
        beyond = beyond + jnp.sum(past, axis=1, keepdims=True)
        spill = jnp.where(late < extra, late + half, -1.0)
        pos[:, b * TILE:(b + 1) * TILE] = jnp.where(past > 0.0, spill, base + rank)
    flags[eights(0), :] = jnp.broadcast_to(jnp.where(beyond > extra, 1.0, 0.0), (8, 128))

    tag8 = jnp.broadcast_to(((lab & 3) + 1).astype(F32), (8, rows)).astype(BF16)
    full8 = jnp.broadcast_to((lab + 1).astype(F32), (8, rows)).astype(BF16)
    lane = lax.broadcasted_iota(jnp.int32, (8, 128), 1)
    index = (lax.broadcasted_iota(jnp.int32, (chunks, 128), 0) * 128
             + lax.broadcasted_iota(jnp.int32, (chunks, 128), 1))
    contract = (((1,), (1,)), ((), ()))

    def picks(t, count=TILE):
        ids = (lax.broadcasted_iota(jnp.int32, (count, rows), 0) + t * TILE).astype(F32)
        return jnp.where(ids == pos[0:1, :], 1.0, 0.0).astype(BF16)

    def own(matrix, k):
        low = k * direct + k // (n // 2) * gap
        return jnp.where((index >= low) & (index < low + direct), matrix, 0.0)

    def lanes(piece, j):
        return jnp.where((lane >= j * extra) & (lane < (j + 1) * extra), piece, 0.0)

    over_tile = half // TILE
    sel = picks(over_tile, 128)
    send[half:half + 128, :] = jnp.dot(sel, unit[...], preferred_element_type=F32).astype(BF16)
    labels0 = lax.dot_general(full8, sel, contract, preferred_element_type=F32)
    labels0 = lanes(labels0, 0)
    otag1[0:8, :] = labels0
    for j in range(1, layer):
        ssend1[j * 8:j * 8 + 8, :] = pltpu.roll(labels0, j * extra, 1)
    recv[half:half + extra, :] = send[half:half + extra, :]
    pl.semaphore_wait(barrier, everyone - 1)
    for j in range(1, layer):
        one_rows(j).start()
        one_tags(j).start()

    @pl.loop(1, everyone)
    def _(q):
        tell(q).start()

    mtag[...] = jnp.zeros_like(mtag)

    def pack(t):
        sel = picks(t)
        send[tile_of(t), :] = jnp.dot(sel, unit[...], preferred_element_type=F32).astype(BF16)
        tags = lax.dot_general(tag8, sel, contract, preferred_element_type=F32)
        mtag[2 * t:2 * t + 1, :] = tags[0:1, :128]
        mtag[2 * t + 1:2 * t + 2, :] = tags[0:1, 128:]

    low_tiles = half // TILE
    packed = list(range(low_tiles)) + list(range(tiles - low_tiles, tiles))

    def start_of(k):
        return k * direct + k // (n // 2) * gap

    ready = 0
    for t in packed:
        pack(t)
        if t == 0:
            recv[0:direct, :] = send[0:direct, :]
        while ready < n and start_of(ready) + direct <= (t + 1) * TILE:
            if ready > 0:
                go_rows(ready).start()
            ready += 1

    every = mtag[...]
    tsum[...] = own(every, 0)

    @pl.loop(1, n)
    def _(k):
        stag[marks(k), :] = own(every, k)
        go_tags(k).start()

    for j in range(1, layer):
        one_rows(j).wait_recv()
        one_tags(j).wait_recv()
    otag2[0:8, :] = otag1[0:8, :] + otag1[8:16, :] + otag1[16:24, :] + otag1[24:32, :]
    for i in range(1, layer):
        two_rows(i).start()
        two_tags(i).start()

    pos_t[...] = jnp.broadcast_to(pos[0:1, :], (128, rows)).T

    def note(t, both):
        both = jnp.broadcast_to(both, (8, TILE))
        ktag[t * 8:t * 8 + 8, :] = jnp.where(both > 0.0, both, -1.0)
        qtag[t * TILE:(t + 1) * TILE, :] = jnp.broadcast_to(both[0:1, :], (128, TILE)).T

    def ends(t):
        if t < low_tiles:
            first, last = t * TILE, (t + 1) * TILE
        else:
            first, last = t * TILE, (t + 1) * TILE
        return [k for k in range(1, n) if first <= start_of(k) < last]

    def arrive(t):
        if low_tiles <= t < tiles - low_tiles:
            chosen = []
            for i in (2 * (t - low_tiles), 2 * (t - low_tiles) + 1):
                if i > 0:
                    two_rows(i).wait_recv()
                    two_tags(i).wait_recv()
                value = otag2[i * 8:i * 8 + 1, :] - (me * CL_DEV).astype(F32)
                chosen.append(jnp.where((value > 0.5) & (value < CL_DEV + 0.5), value, 0.0))
            note(t, jnp.concatenate(chosen, axis=1))
            return
        for k in ends(t):
            go_rows(k).wait_recv()
            go_tags(k).wait_recv()
            tsum[...] += rtag[marks(k), :]
        note(t, jnp.concatenate([tsum[2 * t:2 * t + 1, :], tsum[2 * t + 1:2 * t + 2, :]], axis=1))

    def pair(i, j, fresh=False):
        query, keys = recv[tile_of(i), :], recv[tile_of(j), :]
        sim = lax.dot_general(query, keys, contract, preferred_element_type=F32)
        left = qtag[tile_of(i), :]
        right = ktag[eights(j), :][0:1, :]
        same = jnp.concatenate([left, left], axis=1) == right
        weight = jnp.where(same, jnp.exp2((sim - 1.0) * SCALE), 0.0)
        dens = weight[:, :128] + weight[:, 128:]
        num = jnp.dot(weight.astype(BF16), keys, preferred_element_type=F32)
        if fresh:
            dacc[tile_of(i), :] = dens
            numer[tile_of(i), :] = num
        else:
            dacc[tile_of(i), :] += dens
            numer[tile_of(i), :] += num

    last = tiles - 1
    arrive(0)
    pair(0, 0, True)

    @pl.loop(1, last)
    def _(t):
        for at in range(1, last):
            @pl.when(t == at)
            def _():
                arrive(at)
        pair(t, t, True)

        @pl.loop(0, t)
        def _(i):
            pair(i, t)
            pair(t, i)

    def finish(t):
        dens = jnp.sum(dacc[tile_of(t), :], axis=1, keepdims=True)
        live = qtag[tile_of(t), :] > 0.0
        inv = 1.0 / jnp.where(live, dens, 1.0)
        back[tile_of(t), :] = (
            numer[tile_of(t), :] * jnp.concatenate([inv] * (width // 128), axis=1)).astype(BF16)
        turned = jnp.where(live, dens, 0.0).T
        dmat[pl.ds(2 * t, 1), :] = turned[0:1, :128]
        dmat[pl.ds(2 * t + 1, 1), :] = turned[0:1, 128:]

    arrive(last)
    pair(last, last, True)

    @pl.loop(low_tiles, tiles - low_tiles)
    def _(i):
        pair(i, last)
        finish(i)

    for i in range(1, layer):
        row = half // 128 + i
        ssend2[i * 8:i * 8 + 8, :] = jnp.broadcast_to(dmat[row:row + 1, :], (8, 128))
        three_rows(i).start()
        three_dens(i).start()

    sent = 0
    for t in packed[:-1]:
        pair(t, last)
        finish(t)
        if t == 0:
            home[0:direct, :] = back[0:direct, :]
        while sent < n and start_of(sent) + direct <= (t + 1) * TILE:
            if sent > 0:
                back_rows(sent).start()
            sent += 1

    summed = back[half:half + spare, :].astype(F32)
    here = half // 128
    dens_over = jnp.broadcast_to(dmat[here:here + 1, :], (8, 128))
    for i in range(1, layer):
        three_rows(i).wait_recv()
        three_dens(i).wait_recv()
        summed = summed + obuf[i * spare:(i + 1) * spare, :].astype(F32)
        dens_over = dens_over + oden2[i * 8:i * 8 + 8, :]
    osum[...] = summed.astype(BF16)
    for j in range(1, layer):
        ssend1[(layer + j) * 8:(layer + j) * 8 + 8, :] = pltpu.roll(
            lanes(dens_over, j), 128 - j * extra, 1)
        four_rows(j).start()
        four_dens(j).start()

    @pl.loop(0, last)
    def _(i):
        pair(last, i)

    finish(last)
    for k in range(sent, n):
        back_rows(k).start()

    every_den = dmat[...]
    hsum[...] = own(every_den, 0)

    @pl.loop(1, n)
    def _(k):
        bden[marks(k), :] = own(every_den, k)
        back_dens(k).start()

    home[half + extra:half + gap, :] = jnp.zeros((gap - extra, width), BF16)

    def place(b, t):
        here = pos_t[tile_of(b), :]
        ids = (lax.broadcasted_iota(jnp.int32, (TILE, TILE), 1) + t * TILE).astype(F32)
        sel = jnp.where(ids == jnp.concatenate([here, here], axis=1), 1.0, 0.0).astype(BF16)
        return jnp.dot(sel, home[tile_of(t), :], preferred_element_type=F32)

    def collect(t):
        for k in ends(t):
            back_rows(k).wait_recv()

    collect(0)

    @pl.loop(0, rows // TILE)
    def _(b):
        total[tile_of(b), :] = place(b, 0)

    for t in packed[1:low_tiles]:
        collect(t)

        @pl.loop(0, rows // TILE)
        def _(b):
            total[tile_of(b), :] += place(b, t)

    for j in range(1, layer):
        four_rows(j).wait_recv()
        four_dens(j).wait_recv()
    mine_over = osum[0:extra, :].astype(F32)
    den_over = lanes(dens_over, 0)
    for j in range(1, layer):
        mine_over = mine_over + fin[j * extra:(j + 1) * extra, :].astype(F32)
        den_over = den_over + oden1[j * 8:j * 8 + 8, :]
    home[half:half + extra, :] = mine_over.astype(BF16)

    for t in [over_tile] + packed[low_tiles:-1]:
        if t != over_tile:
            collect(t)

        @pl.loop(0, rows // TILE)
        def _(b):
            total[tile_of(b), :] += place(b, t)

    @pl.loop(1, n)
    def _(k):
        back_dens(k).wait_recv()
        hsum[...] += hden[marks(k), :]

    hsum[here:here + 1, :] = den_over[0:1, :]

    den = jnp.zeros((8, rows), F32)
    for t in packed[:low_tiles] + [over_tile] + packed[low_tiles:]:
        row = jnp.concatenate([hsum[2 * t:2 * t + 1, :], hsum[2 * t + 1:2 * t + 2, :]], axis=1)
        row = jnp.broadcast_to(row, (8, TILE)).astype(BF16)
        den = den + jnp.dot(row, picks(t), preferred_element_type=F32)
    out_dens[...] = den

    collect(last)

    @pl.loop(0, rows // TILE)
    def _(b):
        out[tile_of(b), :] = (total[tile_of(b), :] + place(b, last)).astype(BF16)

    out_flag[...] = flags[eights(0), :]

    @pl.loop(1, everyone)
    def _(q):
        tell(q).wait()
        out_flag[...] = jnp.maximum(out_flag[...], flags[eights(q), :])

    for j in range(1, layer):
        for copy in (one_rows(j), one_tags(j), two_rows(j), two_tags(j),
                     three_rows(j), three_dens(j), four_rows(j), four_dens(j)):
            copy.wait_send()

    @pl.loop(1, n)
    def _(k):
        go_rows(k).wait_send()
        go_tags(k).wait_send()
        back_rows(k).wait_send()
        back_dens(k).wait_send()


def fast(embeds, labels):
    rows, width = embeds.shape
    n, groups = lax.axis_size("wide"), lax.axis_size("groups")
    slots = 2 * rows
    chunks = slots // 128
    cap = slots // n
    vmem = pl.BlockSpec(memory_space=pltpu.VMEM)

    def tall(count):
        return pltpu.VMEM((count, 128), F32)

    def wide(count, kind=BF16):
        return pltpu.VMEM((count, width), kind)

    sems = [pltpu.SemaphoreType.DMA((n,))] * 8 + [pltpu.SemaphoreType.DMA((4,))] * 16
    sems = sems + [pltpu.SemaphoreType.DMA((groups * n,))] * 2
    return pl.pallas_call(
        functools.partial(fast_kernel, n, groups),
        out_shape=(jax.ShapeDtypeStruct((rows, width), BF16),
                   jax.ShapeDtypeStruct((8, rows), F32),
                   jax.ShapeDtypeStruct((8, 128), F32)),
        in_specs=[vmem, vmem],
        out_specs=(vmem, vmem, vmem),
        scratch_shapes=[
            wide(rows), wide(slots), wide(slots), wide(slots), wide(slots),
            wide(slots, F32), wide(rows, F32),
            tall(n * chunks), tall(n * chunks), tall(n * chunks), tall(n * chunks),
            pltpu.VMEM((slots // TILE * 8, TILE), F32),
            tall(slots), tall(slots),
            pltpu.VMEM((8, rows), F32), tall(rows),
            tall(chunks), tall(chunks), tall(chunks), tall(chunks),
            tall(32), tall(32), tall(32), tall(32),
            wide(cap * 4), wide(cap), wide(cap), tall(64), tall(32), tall(groups * n * 8),
        ] + sems,
        compiler_params=pltpu.CompilerParams(
            collective_id=1, has_side_effects=True, vmem_limit_bytes=52 * 1024 * 1024),
        cost_estimate=pl.CostEstimate(
            flops=4 * slots * slots * width + 8 * rows * slots * width,
            bytes_accessed=4 * rows * width, transcendentals=slots * slots),
    )(embeds, labels)


def plain(embeds, labels):
    rows, width = embeds.shape
    n = lax.axis_size("wide")
    slots = 2 * rows
    vmem = pl.BlockSpec(memory_space=pltpu.VMEM)
    average, dens = pl.pallas_call(
        functools.partial(kernel, n),
        out_shape=(jax.ShapeDtypeStruct((rows, width), BF16),
                   jax.ShapeDtypeStruct((8, rows), F32)),
        in_specs=[vmem, vmem],
        out_specs=(vmem, vmem),
        scratch_shapes=[
            pltpu.VMEM((rows, width), BF16),
            pltpu.VMEM((slots, width), BF16),
            pltpu.VMEM((slots, width), BF16),
            pltpu.VMEM((slots, width), BF16),
            pltpu.VMEM((slots, width), BF16),
            pltpu.VMEM((slots, width), F32),
            pltpu.VMEM((rows, width), F32),
            pltpu.VMEM((n * 8, 128), F32),
            pltpu.VMEM((n * 8, 128), F32),
            pltpu.VMEM((n * 8, 128), F32),
            pltpu.VMEM((n * 8, 128), F32),
            pltpu.VMEM((slots // TILE * 8, TILE), F32),
            pltpu.VMEM((slots, 128), F32),
            pltpu.VMEM((slots, 128), F32),
            pltpu.VMEM((8, rows), F32),
            pltpu.VMEM((rows, 128), F32),
        ] + [pltpu.SemaphoreType.DMA((n,))] * 8,
        compiler_params=pltpu.CompilerParams(
            collective_id=0, has_side_effects=True, vmem_limit_bytes=52 * 1024 * 1024),
        cost_estimate=pl.CostEstimate(
            flops=4 * slots * slots * width + 8 * rows * slots * width,
            bytes_accessed=4 * rows * width, transcendentals=slots * slots),
    )(embeds, labels)
    return average, dens


def per_device(embeds, labels):
    rows = embeds.shape[0]
    line = labels.reshape(1, rows)
    if lax.axis_size("wide") == 16 and 2 * rows // 16 == 128:
        average, dens, flag = fast(embeds, line)
        average, dens = lax.cond(
            flag[0, 0] > 0.0, lambda: tuple(plain(embeds, line)), lambda: (average, dens))
    else:
        average, dens = plain(embeds, line)
    return average, dens[0].astype(BF16)


def solution(mesh):
    placed = (P(("groups", "wide"), None), P(("groups", "wide")))
    return jax.shard_map(
        per_device,
        mesh=mesh,
        in_specs=placed,
        out_specs=(P(("groups", "wide"), None), P(("groups", "wide"))),
        check_vma=False,
    )
```

```python
import functools
import math

import jax
import jax.numpy as jnp
from jax import lax
from jax.experimental import pallas as pl
from jax.experimental.pallas import tpu as pltpu
from jax.sharding import PartitionSpec as P

CL_DEV = 4
TAU = 0.2
SCALE = math.log2(math.e) / TAU
TILE = 256
F32 = jnp.float32
BF16 = jnp.bfloat16


def kernel(n, embeds, labels, out, out_dens,
           unit, send, recv, back, home, numer, total,
           stag, rtag, bden, hden, ktag, qtag, dacc, pos, pos_t,
           s_rows, r_rows, s_tags, r_tags, s_back, r_back, s_den, r_den):
    rows, width = embeds.shape
    cap = 2 * rows // n
    slots = n * cap
    tiles = slots // TILE
    per_tile = TILE // cap
    per_lane = 128 // cap
    me = lax.axis_index("wide")

    barrier = pltpu.get_barrier_semaphore()

    @pl.loop(1, n)
    def _(k):
        pl.semaphore_signal(barrier, inc=1, device_id={"wide": lax.rem(me + k, n)},
                            device_id_type=pl.DeviceIdType.MESH)

    def to_dest(k):
        return {"wide": lax.rem(me + k, n)}

    def to_source(k):
        return {"wide": lax.rem(me - k + n, n)}

    def slot_rows(k):
        return pl.ds(pl.multiple_of(k * cap, cap), cap)

    def slot_tags(k):
        return pl.ds(pl.multiple_of(k * 8, 8), 8)

    def remote(src, dst, ssem, rsem, where):
        return pltpu.make_async_remote_copy(
            src_ref=src, dst_ref=dst, send_sem=ssem, recv_sem=rsem,
            device_id=where, device_id_type=pl.DeviceIdType.MESH)

    def go_rows(k):
        return remote(send.at[slot_rows(k)], recv.at[slot_rows(k)], s_rows.at[k], r_rows.at[k], to_dest(k))

    def go_tags(k):
        return remote(stag.at[slot_tags(k)], rtag.at[slot_tags(k)], s_tags.at[k], r_tags.at[k], to_dest(k))

    def back_rows(k):
        return remote(back.at[slot_rows(k)], home.at[slot_rows(k)], s_back.at[k], r_back.at[k], to_source(k))

    def back_dens(k):
        return remote(bden.at[slot_tags(k)], hden.at[slot_tags(k)], s_den.at[k], r_den.at[k], to_source(k))

    def tile_of(t):
        return pl.ds(pl.multiple_of(t * TILE, TILE), TILE)

    @pl.loop(0, rows // 128)
    def _(b):
        at = pl.ds(pl.multiple_of(b * 128, 128), 128)
        x = embeds[at, :].astype(F32)
        inside = jnp.sum(x * x, axis=1, keepdims=True) + 1e-06
        unit[at, :] = (x * lax.rsqrt(inside)).astype(BF16)

    lab = labels[...]
    ahead = (lab >> 2) - me
    ahead = jnp.where(ahead < 0, ahead + n, ahead)
    tag = ((lab & 3) + 1).astype(F32)
    which = lax.broadcasted_iota(jnp.int32, (n, TILE), 0)
    before = (lax.broadcasted_iota(jnp.int32, (TILE, TILE), 0)
              < lax.broadcasted_iota(jnp.int32, (TILE, TILE), 1)).astype(F32).astype(BF16)
    running = jnp.zeros((n, 1), F32)
    for b in range(rows // TILE):
        piece = ahead[:, b * TILE:(b + 1) * TILE]
        hot = (jnp.broadcast_to(piece, (n, TILE)) == which).astype(F32)
        rank = jnp.dot(hot.astype(BF16), before, preferred_element_type=F32) + running
        running = running + jnp.sum(hot, axis=1, keepdims=True)
        rank = jnp.sum(hot * rank, axis=0, keepdims=True)
        pos[:, b * TILE:(b + 1) * TILE] = jnp.broadcast_to(
            rank + (piece * cap).astype(F32), (8, TILE))

    tag8 = jnp.broadcast_to(tag, (8, rows)).astype(BF16)
    lane = lax.broadcasted_iota(jnp.int32, (8, 128), 1)

    def picks(t):
        ids = (lax.broadcasted_iota(jnp.int32, (TILE, rows), 0) + t * TILE).astype(F32)
        return jnp.where(ids == pos[0:1, :], 1.0, 0.0).astype(BF16)

    def own_lanes(piece, j):
        if per_lane == 1:
            return piece
        low = (j % per_lane) * cap
        return jnp.where((lane >= low) & (lane < low + cap), piece, 0.0)

    def pack(t):
        sel = picks(t)
        send[tile_of(t), :] = jnp.dot(sel, unit[...], preferred_element_type=F32).astype(BF16)
        tags = lax.dot_general(tag8, sel, (((1,), (1,)), ((), ())), preferred_element_type=F32)
        for j in range(per_tile):
            at = j // per_lane * 128
            stag[slot_tags(t * per_tile + j), :] = own_lanes(tags[:, at:at + 128], j)

    def launch(t, first):
        for j in range(first, per_tile):
            go_rows(t * per_tile + j).start()
            go_tags(t * per_tile + j).start()

    pack(0)
    pl.semaphore_wait(barrier, n - 1)
    launch(0, 1)
    recv[0:cap, :] = send[0:cap, :]
    rtag[0:8, :] = stag[0:8, :]

    @pl.loop(1, tiles)
    def _(t):
        pack(t)
        launch(t, 0)

    pos_t[...] = jnp.broadcast_to(pos[0:1, :], (128, rows)).T

    def arrive(t, first):
        for j in range(first, per_tile):
            go_rows(t * per_tile + j).wait_recv()
            go_tags(t * per_tile + j).wait_recv()
        halves = []
        for h in range(TILE // 128):
            tags = rtag[slot_tags(t * per_tile + h * per_lane), :]
            for j in range(1, per_lane):
                tags = tags + rtag[slot_tags(t * per_tile + h * per_lane + j), :]
            halves.append(tags)
        both = jnp.concatenate(halves, axis=1)
        ktag[pl.ds(pl.multiple_of(t * 8, 8), 8), :] = jnp.where(both > 0.0, both, -1.0)
        qtag[tile_of(t), :] = jnp.broadcast_to(both[0:1, :], (128, TILE)).T

    def pair(i, j, fresh=False):
        query, keys = recv[tile_of(i), :], recv[tile_of(j), :]
        sim = lax.dot_general(query, keys, (((1,), (1,)), ((), ())), preferred_element_type=F32)
        left = qtag[tile_of(i), :]
        right = ktag[pl.ds(pl.multiple_of(j * 8, 8), 8), :][0:1, :]
        same = jnp.concatenate([left, left], axis=1) == right
        weight = jnp.where(same, jnp.exp2((sim - 1.0) * SCALE), 0.0)
        dens = weight[:, :128] + weight[:, 128:]
        num = jnp.dot(weight.astype(BF16), keys, preferred_element_type=F32)
        if fresh:
            dacc[tile_of(i), :] = dens
            numer[tile_of(i), :] = num
        else:
            dacc[tile_of(i), :] += dens
            numer[tile_of(i), :] += num

    arrive(0, 1)
    pair(0, 0, True)

    @pl.loop(1, tiles - 1)
    def _(t):
        arrive(t, 0)
        pair(t, t, True)

        @pl.loop(0, t)
        def _(i):
            pair(i, t)
            pair(t, i)

    def finish(t):
        dens = jnp.sum(dacc[tile_of(t), :], axis=1, keepdims=True)
        dens = jnp.where(qtag[tile_of(t), :] > 0.0, dens, 1.0)
        inv = 1.0 / dens
        back[tile_of(t), :] = (
            numer[tile_of(t), :] * jnp.concatenate([inv] * (width // 128), axis=1)).astype(BF16)
        turned = dens.T[0:8, :]
        for j in range(per_tile):
            at = j // per_lane * 128
            bden[slot_tags(t * per_tile + j), :] = own_lanes(turned[:, at:at + 128], j)

    def give(t, first):
        for j in range(first, per_tile):
            back_rows(t * per_tile + j).start()
            back_dens(t * per_tile + j).start()

    last = tiles - 1
    arrive(last, 0)
    pair(last, last, True)
    pair(0, last)
    finish(0)
    give(0, 1)
    home[0:cap, :] = back[0:cap, :]
    hden[0:8, :] = bden[0:8, :]

    @pl.loop(1, last)
    def _(i):
        pair(i, last)
        finish(i)
        give(i, 0)

    @pl.loop(0, last)
    def _(i):
        pair(last, i)

    finish(last)
    give(last, 0)

    def collect(t, first):
        for j in range(first, per_tile):
            back_rows(t * per_tile + j).wait_recv()
            back_dens(t * per_tile + j).wait_recv()
        halves = []
        for h in range(TILE // 128):
            den = hden[slot_tags(t * per_tile + h * per_lane), :]
            for j in range(1, per_lane):
                den = den + hden[slot_tags(t * per_tile + h * per_lane + j), :]
            halves.append(den)
        den = jnp.concatenate(halves, axis=1).astype(BF16)
        den = jnp.dot(den, picks(t), preferred_element_type=F32)
        came = home[tile_of(t), :]
        ids = (lax.broadcasted_iota(jnp.int32, (TILE, TILE), 1) + t * TILE).astype(F32)
        return came, ids, den

    def place(b, came, ids):
        here = pos_t[tile_of(b), :]
        sel = jnp.where(ids == jnp.concatenate([here, here], axis=1), 1.0, 0.0).astype(BF16)
        return jnp.dot(sel, came, preferred_element_type=F32)

    came, ids, den = collect(0, 1)
    out_dens[...] = den
    for b in range(rows // TILE):
        total[tile_of(b), :] = place(b, came, ids)

    @pl.loop(1, last)
    def _(t):
        came, ids, den = collect(t, 0)
        out_dens[...] += den
        for b in range(rows // TILE):
            total[tile_of(b), :] += place(b, came, ids)

    came, ids, den = collect(last, 0)
    out_dens[...] += den
    for b in range(rows // TILE):
        out[tile_of(b), :] = (total[tile_of(b), :] + place(b, came, ids)).astype(BF16)

    @pl.loop(1, n)
    def _(k):
        go_rows(k).wait_send()
        go_tags(k).wait_send()
        back_rows(k).wait_send()
        back_dens(k).wait_send()


def fast_kernel(n, groups, embeds, labels, out, out_dens, out_flag,
                unit, send, recv, back, home, numer, total,
                stag, rtag, bden, hden, ktag, qtag, dacc, drow, pos, pos_t,
                mtag, tsum, dmat, hsum, otag1, otag2, oden2, oden1, obuf, osum, fin, ssend1, ssend2, flags,
                s_rows, r_rows, s_tags, r_tags, s_back, r_back, s_den, r_den,
                s_o1, r_o1, s_o1t, r_o1t, s_o2, r_o2, s_o2t, r_o2t,
                s_b2, r_b2, s_b2d, r_b2d, s_b1, r_b1, s_b1d, r_b1d, s_f, r_f):
    rows, width = embeds.shape
    cap = 2 * rows // n
    direct = 3 * cap // 4
    extra = cap // 4
    layer = 4
    half = n // 2 * direct
    gap = n * extra
    slots = 2 * rows
    tiles = slots // TILE
    spare = gap // layer
    chunks = slots // 128
    me = lax.axis_index("wide")
    mine = lax.axis_index("groups") * n + me
    everyone = groups * n
    floor, spot = me // layer, lax.rem(me, layer)

    barrier = pltpu.get_barrier_semaphore()

    def nth(q):
        who = lax.rem(q + everyone, everyone)
        return {"groups": who // n, "wide": lax.rem(who, n)}

    @pl.loop(1, everyone)
    def _(q):
        pl.semaphore_signal(barrier, inc=1, device_id=nth(mine + q), device_id_type=pl.DeviceIdType.MESH)

    def to_dest(k):
        return {"wide": lax.rem(me + k, n)}

    def to_source(k):
        return {"wide": lax.rem(me - k + n, n)}

    def across(i):
        return {"wide": floor * layer + lax.rem(spot + i + layer, layer)}

    def slot_rows(k):
        return pl.ds(pl.multiple_of(k * direct + k // (n // 2) * gap, 32), direct)

    def eights(k):
        return pl.ds(pl.multiple_of(k * 8, 8), 8)

    def marks(k):
        return pl.ds(pl.multiple_of(k * chunks, 8), chunks)

    def tile_of(t):
        return pl.ds(pl.multiple_of(t * TILE, TILE), TILE)

    def over(i):
        return pl.ds(half + i * spare, spare)

    def part(j):
        return pl.ds(half + j * extra, extra)

    def remote(src, dst, ssem, rsem, where):
        return pltpu.make_async_remote_copy(
            src_ref=src, dst_ref=dst, send_sem=ssem, recv_sem=rsem,
            device_id=where, device_id_type=pl.DeviceIdType.MESH)

    def go_rows(k):
        return remote(send.at[slot_rows(k)], recv.at[slot_rows(k)], s_rows.at[k], r_rows.at[k], to_dest(k))

    def go_tags(k):
        return remote(stag.at[marks(k)], rtag.at[marks(k)], s_tags.at[k], r_tags.at[k], to_dest(k))

    def back_rows(k):
        return remote(back.at[slot_rows(k)], home.at[slot_rows(k)], s_back.at[k], r_back.at[k], to_source(k))

    def back_dens(k):
        return remote(bden.at[marks(k)], hden.at[marks(k)], s_den.at[k], r_den.at[k], to_source(k))

    def one_rows(j):
        return remote(send.at[part(0)], recv.at[part(j)], s_o1.at[j], r_o1.at[j], to_dest(layer * j))

    def one_tags(j):
        return remote(ssend1.at[eights(j)], otag1.at[eights(j)], s_o1t.at[j], r_o1t.at[j], to_dest(layer * j))

    def two_rows(i):
        return remote(recv.at[over(0)], recv.at[over(i)], s_o2.at[i], r_o2.at[i], across(i))

    def two_tags(i):
        return remote(otag2.at[eights(0)], otag2.at[eights(i)], s_o2t.at[i], r_o2t.at[i], across(i))

    def three_rows(i):
        return remote(back.at[over(i)], obuf.at[pl.ds(i * spare, spare)], s_b2.at[i], r_b2.at[i], across(-i))

    def three_dens(i):
        return remote(ssend2.at[eights(i)], oden2.at[eights(i)], s_b2d.at[i], r_b2d.at[i], across(-i))

    def four_rows(j):
        return remote(osum.at[pl.ds(j * extra, extra)], fin.at[pl.ds(j * extra, extra)],
                      s_b1.at[j], r_b1.at[j], to_source(layer * j))

    def four_dens(j):
        return remote(ssend1.at[eights(layer + j)], oden1.at[eights(j)], s_b1d.at[j], r_b1d.at[j],
                      to_source(layer * j))

    def tell(q):
        return remote(flags.at[eights(0)], flags.at[eights(q)], s_f.at[q], r_f.at[q], nth(mine + q))

    @pl.loop(0, rows // 128)
    def _(b):
        at = pl.ds(pl.multiple_of(b * 128, 128), 128)
        x = embeds[at, :].astype(F32)
        inside = jnp.sum(x * x, axis=1, keepdims=True) + 1e-06
        unit[at, :] = (x * lax.rsqrt(inside)).astype(BF16)

    lab = labels[...]
    ahead = (lab >> 2) - me
    ahead = jnp.where(ahead < 0, ahead + n, ahead)
    which = lax.broadcasted_iota(jnp.int32, (n, TILE), 0)
    before = (lax.broadcasted_iota(jnp.int32, (TILE, TILE), 0)
              < lax.broadcasted_iota(jnp.int32, (TILE, TILE), 1)).astype(F32).astype(BF16)
    running = jnp.zeros((n, 1), F32)
    beyond = jnp.zeros((8, 1), F32)
    for b in range(rows // TILE):
        piece = ahead[:, b * TILE:(b + 1) * TILE]
        hot = (jnp.broadcast_to(piece, (n, TILE)) == which).astype(F32)
        rank = jnp.dot(hot.astype(BF16), before, preferred_element_type=F32) + running
        running = running + jnp.sum(hot, axis=1, keepdims=True)
        rank = jnp.broadcast_to(jnp.sum(hot * rank, axis=0, keepdims=True), (8, TILE))
        base = jnp.broadcast_to(
            (piece * direct + jnp.where(piece >= n // 2, gap, 0)).astype(F32), (8, TILE))
        past = jnp.where(rank >= direct, 1.0, 0.0)
        late = jnp.dot(past.astype(BF16), before, preferred_element_type=F32) + beyond
        beyond = beyond + jnp.sum(past, axis=1, keepdims=True)
        spill = jnp.where(late < extra, late + half, -1.0)
        pos[:, b * TILE:(b + 1) * TILE] = jnp.where(past > 0.0, spill, base + rank)
    flags[eights(0), :] = jnp.broadcast_to(jnp.where(beyond > extra, 1.0, 0.0), (8, 128))

    tag8 = jnp.broadcast_to(((lab & 3) + 1).astype(F32), (8, rows)).astype(BF16)
    full8 = jnp.broadcast_to((lab + 1).astype(F32), (8, rows)).astype(BF16)
    lane = lax.broadcasted_iota(jnp.int32, (8, 128), 1)
    index = (lax.broadcasted_iota(jnp.int32, (chunks, 128), 0) * 128
             + lax.broadcasted_iota(jnp.int32, (chunks, 128), 1))
    contract = (((1,), (1,)), ((), ()))

    def picks(t, count=TILE):
        ids = (lax.broadcasted_iota(jnp.int32, (count, rows), 0) + t * TILE).astype(F32)
        return jnp.where(ids == pos[0:1, :], 1.0, 0.0).astype(BF16)

    def own(matrix, k):
        low = k * direct + k // (n // 2) * gap
        return jnp.where((index >= low) & (index < low + direct), matrix, 0.0)

    def lanes(piece, j):
        return jnp.where((lane >= j * extra) & (lane < (j + 1) * extra), piece, 0.0)

    over_tile = half // TILE
    sel = picks(over_tile, 128)
    send[half:half + 128, :] = jnp.dot(sel, unit[...], preferred_element_type=F32).astype(BF16)
    labels0 = lax.dot_general(full8, sel, contract, preferred_element_type=F32)
    labels0 = lanes(labels0, 0)
    otag1[0:8, :] = labels0
    for j in range(1, layer):
        ssend1[j * 8:j * 8 + 8, :] = pltpu.roll(labels0, j * extra, 1)
    recv[half:half + extra, :] = send[half:half + extra, :]
    pl.semaphore_wait(barrier, everyone - 1)
    for j in range(1, layer):
        one_rows(j).start()
        one_tags(j).start()

    @pl.loop(1, everyone)
    def _(q):
        tell(q).start()

    mtag[...] = jnp.zeros_like(mtag)

    def pack(t):
        sel = picks(t)
        send[tile_of(t), :] = jnp.dot(sel, unit[...], preferred_element_type=F32).astype(BF16)
        tags = lax.dot_general(tag8, sel, contract, preferred_element_type=F32)
        mtag[2 * t:2 * t + 1, :] = tags[0:1, :128]
        mtag[2 * t + 1:2 * t + 2, :] = tags[0:1, 128:]

    low_tiles = half // TILE
    packed = list(range(low_tiles)) + list(range(tiles - low_tiles, tiles))

    def start_of(k):
        return k * direct + k // (n // 2) * gap

    ready = 0
    for t in packed:
        pack(t)
        if t == 0:
            recv[0:direct, :] = send[0:direct, :]
        while ready < n and start_of(ready) + direct <= (t + 1) * TILE:
            if ready > 0:
                stag[ready * chunks:(ready + 1) * chunks, :] = own(mtag[...], ready)
                go_tags(ready).start()
                go_rows(ready).start()
            ready += 1
        if t == low_tiles - 1:
            for j in range(1, layer):
                one_rows(j).wait_recv()
                one_tags(j).wait_recv()
            otag2[0:8, :] = otag1[0:8, :] + otag1[8:16, :] + otag1[16:24, :] + otag1[24:32, :]
            for i in range(1, layer):
                two_rows(i).start()
                two_tags(i).start()

    tsum[...] = own(mtag[...], 0)

    pos_t[...] = jnp.broadcast_to(pos[0:1, :], (128, rows)).T

    def note(t, both):
        both = jnp.broadcast_to(both, (8, TILE))
        ktag[t * 8:t * 8 + 8, :] = jnp.where(both > 0.0, both, -1.0)
        qtag[t * TILE:(t + 1) * TILE, :] = jnp.broadcast_to(both[0:1, :], (128, TILE)).T

    def ends(t):
        if t < low_tiles:
            first, last = t * TILE, (t + 1) * TILE
        else:
            first, last = t * TILE, (t + 1) * TILE
        return [k for k in range(1, n) if first <= start_of(k) < last]

    def arrive(t):
        if low_tiles <= t < tiles - low_tiles:
            chosen = []
            for i in (2 * (t - low_tiles), 2 * (t - low_tiles) + 1):
                if i > 0:
                    two_rows(i).wait_recv()
                    two_tags(i).wait_recv()
                value = otag2[i * 8:i * 8 + 1, :] - (me * CL_DEV).astype(F32)
                chosen.append(jnp.where((value > 0.5) & (value < CL_DEV + 0.5), value, 0.0))
            note(t, jnp.concatenate(chosen, axis=1))
            return
        for k in ends(t):
            go_rows(k).wait_recv()
            go_tags(k).wait_recv()
            tsum[...] += rtag[marks(k), :]
        note(t, jnp.concatenate([tsum[2 * t:2 * t + 1, :], tsum[2 * t + 1:2 * t + 2, :]], axis=1))

    def pair(i, j, fresh=False):
        query, keys = recv[tile_of(i), :], recv[tile_of(j), :]
        sim = lax.dot_general(query, keys, contract, preferred_element_type=F32)
        left = qtag[tile_of(i), :]
        right = ktag[eights(j), :][0:1, :]
        same = jnp.concatenate([left, left], axis=1) == right
        weight = jnp.where(same, jnp.exp2((sim - 1.0) * SCALE), 0.0)
        dens = weight[:, :128] + weight[:, 128:]
        num = jnp.dot(weight.astype(BF16), keys, preferred_element_type=F32)
        if fresh:
            dacc[tile_of(i), :] = dens
            numer[tile_of(i), :] = num
        else:
            dacc[tile_of(i), :] += dens
            numer[tile_of(i), :] += num

    def both(i, t):
        query, keys = recv[tile_of(i), :], recv[tile_of(t), :]
        sim = lax.dot_general(query, keys, contract, preferred_element_type=F32)
        left = qtag[tile_of(i), :]
        right = ktag[eights(t), :][0:1, :]
        same = jnp.concatenate([left, left], axis=1) == right
        weight = jnp.where(same, jnp.exp2((sim - 1.0) * SCALE), 0.0)
        rounded = weight.astype(BF16)
        num_i = jnp.dot(rounded, keys, preferred_element_type=F32)
        num_t = lax.dot_general(rounded, query, (((0,), (0,)), ((), ())), preferred_element_type=F32)
        old_i, old_t = numer[tile_of(i), :], numer[tile_of(t), :]
        dacc[tile_of(i), :] += weight[:, :128] + weight[:, 128:]
        drow[eights(t), :] += jnp.sum(weight.reshape(TILE // 8, 8, TILE), axis=0)
        numer[tile_of(i), :] = old_i + num_i
        numer[tile_of(t), :] = old_t + num_t

    drow[...] = jnp.zeros_like(drow)
    last = tiles - 1
    arrive(0)
    pair(0, 0, True)

    @pl.loop(1, last)
    def _(t):
        for at in range(1, last):
            @pl.when(t == at)
            def _():
                arrive(at)
        pair(t, t, True)

        @pl.loop(0, t)
        def _(i):
            both(i, t)

    def finish(t):
        down = jnp.sum(drow[eights(t), :], axis=0, keepdims=True)
        dens = (jnp.sum(dacc[tile_of(t), :], axis=1, keepdims=True)
                + jnp.broadcast_to(down, (128, TILE)).T)
        live = qtag[tile_of(t), :] > 0.0
        inv = 1.0 / jnp.where(live, dens, 1.0)
        back[tile_of(t), :] = (
            numer[tile_of(t), :] * jnp.concatenate([inv] * (width // 128), axis=1)).astype(BF16)
        turned = jnp.where(live, dens, 0.0).T
        dmat[pl.ds(2 * t, 1), :] = turned[0:1, :128]
        dmat[pl.ds(2 * t + 1, 1), :] = turned[0:1, 128:]

    arrive(last)
    pair(last, last, True)

    @pl.loop(low_tiles, tiles - low_tiles)
    def _(i):
        both(i, last)
        finish(i)

    for i in range(1, layer):
        row = half // 128 + i
        ssend2[i * 8:i * 8 + 8, :] = jnp.broadcast_to(dmat[row:row + 1, :], (8, 128))
        three_rows(i).start()
        three_dens(i).start()

    sent = 0
    for t in packed[:-1]:
        both(t, last)
        finish(t)
        if t == 0:
            home[0:direct, :] = back[0:direct, :]
        while sent < n and start_of(sent) + direct <= (t + 1) * TILE:
            if sent > 0:
                back_rows(sent).start()
            sent += 1

    summed = back[half:half + spare, :].astype(F32)
    here = half // 128
    dens_over = jnp.broadcast_to(dmat[here:here + 1, :], (8, 128))
    for i in range(1, layer):
        three_rows(i).wait_recv()
        three_dens(i).wait_recv()
        summed = summed + obuf[i * spare:(i + 1) * spare, :].astype(F32)
        dens_over = dens_over + oden2[i * 8:i * 8 + 8, :]
    osum[...] = summed.astype(BF16)
    for j in range(1, layer):
        ssend1[(layer + j) * 8:(layer + j) * 8 + 8, :] = pltpu.roll(
            lanes(dens_over, j), 128 - j * extra, 1)
        four_rows(j).start()
        four_dens(j).start()

    finish(last)
    for k in range(sent, n):
        back_rows(k).start()

    every_den = dmat[...]
    hsum[...] = own(every_den, 0)

    @pl.loop(1, n)
    def _(k):
        bden[marks(k), :] = own(every_den, k)
        back_dens(k).start()

    home[half + extra:half + gap, :] = jnp.zeros((gap - extra, width), BF16)

    def place(b, t):
        here = pos_t[tile_of(b), :]
        ids = (lax.broadcasted_iota(jnp.int32, (TILE, TILE), 1) + t * TILE).astype(F32)
        sel = jnp.where(ids == jnp.concatenate([here, here], axis=1), 1.0, 0.0).astype(BF16)
        return jnp.dot(sel, home[tile_of(t), :], preferred_element_type=F32)

    def collect(t):
        for k in ends(t):
            back_rows(k).wait_recv()

    collect(0)

    for b in range(rows // TILE):
        total[tile_of(b), :] = place(b, 0)

    for t in packed[1:low_tiles]:
        collect(t)

        for b in range(rows // TILE):
            total[tile_of(b), :] += place(b, t)

    for j in range(1, layer):
        four_rows(j).wait_recv()
        four_dens(j).wait_recv()
    mine_over = osum[0:extra, :].astype(F32)
    den_over = lanes(dens_over, 0)
    for j in range(1, layer):
        mine_over = mine_over + fin[j * extra:(j + 1) * extra, :].astype(F32)
        den_over = den_over + oden1[j * 8:j * 8 + 8, :]
    home[half:half + extra, :] = mine_over.astype(BF16)

    for t in [over_tile] + packed[low_tiles:-1]:
        if t != over_tile:
            collect(t)

        for b in range(rows // TILE):
            total[tile_of(b), :] += place(b, t)

    @pl.loop(1, n)
    def _(k):
        back_dens(k).wait_recv()
        hsum[...] += hden[marks(k), :]

    hsum[here:here + 1, :] = den_over[0:1, :]

    den = jnp.zeros((8, rows), F32)
    for t in packed[:low_tiles] + [over_tile] + packed[low_tiles:]:
        row = jnp.concatenate([hsum[2 * t:2 * t + 1, :], hsum[2 * t + 1:2 * t + 2, :]], axis=1)
        row = jnp.broadcast_to(row, (8, TILE)).astype(BF16)
        den = den + jnp.dot(row, picks(t), preferred_element_type=F32)
    out_dens[...] = den

    collect(last)

    for b in range(rows // TILE):
        out[tile_of(b), :] = (total[tile_of(b), :] + place(b, last)).astype(BF16)

    out_flag[...] = flags[eights(0), :]

    @pl.loop(1, everyone)
    def _(q):
        tell(q).wait()
        out_flag[...] = jnp.maximum(out_flag[...], flags[eights(q), :])

    for j in range(1, layer):
        for copy in (one_rows(j), one_tags(j), two_rows(j), two_tags(j),
                     three_rows(j), three_dens(j), four_rows(j), four_dens(j)):
            copy.wait_send()

    @pl.loop(1, n)
    def _(k):
        go_rows(k).wait_send()
        go_tags(k).wait_send()
        back_rows(k).wait_send()
        back_dens(k).wait_send()


def fast(embeds, labels):
    rows, width = embeds.shape
    n, groups = lax.axis_size("wide"), lax.axis_size("groups")
    slots = 2 * rows
    chunks = slots // 128
    cap = slots // n
    vmem = pl.BlockSpec(memory_space=pltpu.VMEM)

    def tall(count):
        return pltpu.VMEM((count, 128), F32)

    def wide(count, kind=BF16):
        return pltpu.VMEM((count, width), kind)

    sems = [pltpu.SemaphoreType.DMA((n,))] * 8 + [pltpu.SemaphoreType.DMA((4,))] * 16
    sems = sems + [pltpu.SemaphoreType.DMA((groups * n,))] * 2
    return pl.pallas_call(
        functools.partial(fast_kernel, n, groups),
        out_shape=(jax.ShapeDtypeStruct((rows, width), BF16),
                   jax.ShapeDtypeStruct((8, rows), F32),
                   jax.ShapeDtypeStruct((8, 128), F32)),
        in_specs=[vmem, vmem],
        out_specs=(vmem, vmem, vmem),
        scratch_shapes=[
            wide(rows), wide(slots), wide(slots), wide(slots), wide(slots),
            wide(slots, F32), wide(rows, F32),
            tall(n * chunks), tall(n * chunks), tall(n * chunks), tall(n * chunks),
            pltpu.VMEM((slots // TILE * 8, TILE), F32),
            tall(slots), tall(slots), pltpu.VMEM((slots // TILE * 8, TILE), F32),
            pltpu.VMEM((8, rows), F32), tall(rows),
            tall(chunks), tall(chunks), tall(chunks), tall(chunks),
            tall(32), tall(32), tall(32), tall(32),
            wide(cap * 4), wide(cap), wide(cap), tall(64), tall(32), tall(groups * n * 8),
        ] + sems,
        compiler_params=pltpu.CompilerParams(
            collective_id=1, has_side_effects=True, vmem_limit_bytes=52 * 1024 * 1024),
        cost_estimate=pl.CostEstimate(
            flops=4 * slots * slots * width + 8 * rows * slots * width,
            bytes_accessed=4 * rows * width, transcendentals=slots * slots),
    )(embeds, labels)


def plain(embeds, labels):
    rows, width = embeds.shape
    n = lax.axis_size("wide")
    slots = 2 * rows
    vmem = pl.BlockSpec(memory_space=pltpu.VMEM)
    average, dens = pl.pallas_call(
        functools.partial(kernel, n),
        out_shape=(jax.ShapeDtypeStruct((rows, width), BF16),
                   jax.ShapeDtypeStruct((8, rows), F32)),
        in_specs=[vmem, vmem],
        out_specs=(vmem, vmem),
        scratch_shapes=[
            pltpu.VMEM((rows, width), BF16),
            pltpu.VMEM((slots, width), BF16),
            pltpu.VMEM((slots, width), BF16),
            pltpu.VMEM((slots, width), BF16),
            pltpu.VMEM((slots, width), BF16),
            pltpu.VMEM((slots, width), F32),
            pltpu.VMEM((rows, width), F32),
            pltpu.VMEM((n * 8, 128), F32),
            pltpu.VMEM((n * 8, 128), F32),
            pltpu.VMEM((n * 8, 128), F32),
            pltpu.VMEM((n * 8, 128), F32),
            pltpu.VMEM((slots // TILE * 8, TILE), F32),
            pltpu.VMEM((slots, 128), F32),
            pltpu.VMEM((slots, 128), F32),
            pltpu.VMEM((8, rows), F32),
            pltpu.VMEM((rows, 128), F32),
        ] + [pltpu.SemaphoreType.DMA((n,))] * 8,
        compiler_params=pltpu.CompilerParams(
            collective_id=0, has_side_effects=True, vmem_limit_bytes=52 * 1024 * 1024),
        cost_estimate=pl.CostEstimate(
            flops=4 * slots * slots * width + 8 * rows * slots * width,
            bytes_accessed=4 * rows * width, transcendentals=slots * slots),
    )(embeds, labels)
    return average, dens


def per_device(embeds, labels):
    rows = embeds.shape[0]
    line = labels.reshape(1, rows)
    if lax.axis_size("wide") == 16 and 2 * rows // 16 == 128:
        average, dens, flag = fast(embeds, line)
        average, dens = lax.cond(
            flag[0, 0] > 0.0, lambda: tuple(plain(embeds, line)), lambda: (average, dens))
    else:
        average, dens = plain(embeds, line)
    return average, dens[0].astype(BF16)


def solution(mesh):
    placed = (P(("groups", "wide"), None), P(("groups", "wide")))
    return jax.shard_map(
        per_device,
        mesh=mesh,
        in_specs=placed,
        out_specs=(P(("groups", "wide"), None), P(("groups", "wide"))),
        check_vma=False,
    )
```
